512 devices in a mesh: mem: 16 (over y, x), tile: 32 (over z, core).
Axes of the slice: x: 4, y: 4, z: 16, core: 2. Of those that a mesh axis runs over, the one named last changes fastest.
Arguments:
- state: float32 [256, 2048, 4, 128], P('mem', 'tile'), may hold values from -6 to 6
- obs_prior: float32 [256, 2048, 128], P('mem', 'tile'), may hold values from -6 to 6
- obs_value: float32 [2048, 128], P('tile'), may hold values from -6 to 6
- obs_prec: float32 [2048, 128], P('tile'), may hold values from 0.05 to 1
- tile_batches: int32 [2048, 6], P('tile'), may hold values from 0 to 2047, as said below
- tile_count: int32 [2048], P('tile'), may hold values from 1 to 6, as said below
- loc_weight: float32 [2048, 6], P('tile'), may hold values from 0.1 to 1
Outputs:
- analysis: float32 [256, 2048, 4, 128], P('mem', 'tile')
The draws below stay inside these ranges and needn't reach their ends.
Inputs may be any that keep to these rules, and one draw needn't show every extreme that they name: `tile_batches`: row t holds 6 different batch numbers (t + o) mod 2048 with |o| <= 16. Only the first tile_count[t] entries of row t of tile_batches and loc_weight are used.
All inputs are finite; a program needn't handle non-finite values.
Results may differ from the reference program's by a relative error of at most 0.0003.
Values sent between devices are 32-bit elements; how exact they have to be, the bound alone decides.
A program may use at most 128 MiB of HBM per device.

```python
import math
import jax
import jax.numpy as jnp
from jax import lax

MEMBERS = 256
FIELDS = 4
POINTS = 128
BATCH_OBS = 128
SLOTS = 6
SWEEPS = 3
TILES = 2048
BATCHES = 2048
REACH = 16


def draw_tile_batches(key, part):
    key = jax.random.fold_in(key, 11)
    width = 2 * REACH + 1
    scores = jax.random.randint(key, (TILES, width), 0, 1000, dtype=jnp.int32) * width + jnp.arange(width, dtype=jnp.int32)[None, :]
    order = jnp.argsort(scores, axis=1)[:, :SLOTS].astype(jnp.int32)
    offsets = order - REACH
    listed = (jnp.arange(TILES, dtype=jnp.int32)[:, None] + offsets) % BATCHES
    return listed.astype(jnp.int32)


def draw_tile_count(key, part):
    key = jax.random.fold_in(key, 23)
    counts = jax.random.randint(key, (TILES,), 1, SLOTS + 1, dtype=jnp.int32)
    counts = counts.at[0].set(SLOTS)
    counts = counts.at[1].set(1)
    return counts.astype(jnp.int32)


def block_levels(key, dims, pieces, least, top_value):
    def one(dim, blocks):
        draws = jax.random.uniform(jax.random.fold_in(jax.random.fold_in(key, 6), dim), (blocks,), jnp.float32, least / len(pieces), top_value / len(pieces))
        return jnp.repeat(jnp.exp(draws), dims[dim] // blocks).reshape((-1,) + (1,) * (len(dims) - dim - 1))

    factor_of = one(*pieces[0])
    for cut in pieces[1:]:
        factor_of = factor_of * one(*cut)
    return factor_of


def gaussian(own_key, shape, spread, most, cuts=(), kind=jnp.bfloat16):
    values = jax.random.normal(own_key, shape, jnp.float32) * spread
    if len(cuts) > 0:
        values = block_levels(own_key, shape, cuts, -0.22, 0.18) * values
    return jnp.clip(values, min=-most, max=most).astype(kind)


def setup_inputs(seed: int = 0) -> dict:
    splits = jax.random.split(jax.random.key(seed), 8)
    state = gaussian(splits[0], (MEMBERS, TILES, FIELDS, POINTS), 1.0, 6.0, ((0, 16), (1, 32)), jnp.float32)
    obs_prior = gaussian(splits[1], (MEMBERS, BATCHES, BATCH_OBS), 1.0, 6.0, ((0, 16), (1, 32)), jnp.float32)
    obs_value = gaussian(splits[2], (BATCHES, BATCH_OBS), 1.0, 6.0, ((0, 32),), jnp.float32)
    obs_prec = jnp.clip(jnp.exp(math.log(1.0) - 2.9957323 * jax.random.uniform(splits[3], (BATCHES, BATCH_OBS), jnp.float32) ** block_levels(splits[3], (BATCHES, BATCH_OBS), ((0, 32),), -0.2, 0.2)), 0.05, 1.0)
    tile_batches = draw_tile_batches(jax.random.fold_in(splits[7], 71), 0)
    tile_count = draw_tile_count(jax.random.fold_in(splits[7], 71), 0)
    loc_weight = jnp.clip(jnp.exp(math.log(1.0) - 2.3025851 * jax.random.uniform(splits[6], (TILES, SLOTS), jnp.float32) ** block_levels(splits[6], (TILES, SLOTS), ((0, 32),), -0.2, 0.2)), 0.1, 1.0)
    return dict(state=state, obs_prior=obs_prior, obs_value=obs_value, obs_prec=obs_prec, tile_batches=tile_batches, tile_count=tile_count, loc_weight=loc_weight)


def finish(xmean, xpert, gram, proj):
    highest = lax.Precision.HIGHEST
    members = xpert.shape[0]
    ident = jnp.eye(members, dtype=jnp.float32)
    amat = (members - 1.0) * ident + gram
    scale = jnp.sqrt(jnp.sum(amat * amat))
    root = amat / scale
    inverse = ident
    for sweep in range(SWEEPS):
        factor = 1.5 * ident - 0.5 * jnp.dot(inverse, root, precision=highest)
        root = jnp.dot(root, factor, precision=highest)
        inverse = jnp.dot(factor, inverse, precision=highest)
    cover = jnp.dot(inverse, inverse, precision=highest) / scale
    wmean = jnp.dot(cover, proj, precision=highest)
    weights = jnp.sqrt((members - 1.0) / scale) * inverse + wmean[:, None]
    flat = xpert.reshape(members, -1)
    moved = jnp.dot(weights.T, flat, precision=highest)
    return xmean + moved.reshape(xpert.shape)

def one_tile(obs_prior, obs_value, obs_prec, tile_state, listed, count, weight):
    highest = lax.Precision.HIGHEST
    prior = jnp.take(obs_prior, listed, axis=1)
    values = jnp.take(obs_value, listed, axis=0)
    precs = jnp.take(obs_prec, listed, axis=0)
    live = (jnp.arange(SLOTS, dtype=jnp.int32) < count).astype(jnp.float32)
    xmean = lax.optimization_barrier(jnp.mean(tile_state, axis=0))
    xpert = tile_state - xmean
    ymean = lax.optimization_barrier(jnp.mean(prior, axis=0))
    ypert = prior - ymean
    innov = values - ymean
    scaled = ypert * (precs * (weight * live)[:, None])
    gram = jnp.einsum('ksb,jsb->kj', scaled, ypert, precision=highest)
    proj = jnp.einsum('ksb,sb->k', scaled, innov, precision=highest)
    return finish(xmean, xpert, gram, proj)

def reference(state, obs_prior, obs_value, obs_prec, tile_batches, tile_count, loc_weight):
    group = math.gcd(TILES, 16)
    blocks = TILES // group
    states = jnp.moveaxis(state, 1, 0).reshape(blocks, group, MEMBERS, FIELDS, POINTS)
    listed = tile_batches.reshape(blocks, group, SLOTS)
    counts = tile_count.reshape(blocks, group)
    weights = loc_weight.reshape(blocks, group, SLOTS)

    def run_block(items):
        return jax.vmap(lambda a, b, c, d: one_tile(obs_prior, obs_value, obs_prec, a, b, c, d))(*items)
    result = lax.map(run_block, (states, listed, counts, weights))
    result = result.reshape(TILES, MEMBERS, FIELDS, POINTS)
    return jnp.moveaxis(result, 0, 1)
```

```python
import jax
import jax.numpy as jnp
from jax import lax
from jax.experimental import pallas as pl
from jax.experimental.pallas import tpu as pltpu
from jax.sharding import PartitionSpec as P

MESH = pl.DeviceIdType.MESH
MEMBERS = 256
SLOTS = 6
PER = 4
WINDOW = 36

F32 = jnp.float32
BF16 = jnp.bfloat16
NN = (((1,), (0,)), ((), ()))
NT = (((1,), (1,)), ((), ()))


def split(x):
    high = x.astype(BF16)
    return high, (x - high.astype(F32)).astype(BF16)


def mxu(a, b, dims=NN):
    return lax.dot_general(a, b, dims, preferred_element_type=F32)


def mul(a, b, dims=NN):
    ah, al = a
    bh, bl = b
    return mxu(ah, bh, dims) + (mxu(ah, bl, dims) + mxu(al, bh, dims))


def transform(gram, proj):
    rows = lax.broadcasted_iota(jnp.int32, (MEMBERS, MEMBERS), 0)
    cols = lax.broadcasted_iota(jnp.int32, (MEMBERS, MEMBERS), 1)
    diag = rows == cols
    ident = diag.astype(F32)
    amat = (MEMBERS - 1.0) * ident + gram
    scale = jnp.sqrt(jnp.sum(amat * amat, keepdims=True))
    root = amat * (1.0 / scale)
    first = 1.5 * ident - 0.5 * root
    root_s = split(root)
    first_s = split(first)
    square = mul(root_s, root_s)
    inner = mul(first_s, split(1.5 * root - 0.5 * square))
    second = 1.5 * ident - 0.5 * inner
    second_s = split(second)
    r = mul(second_s, second_s)
    poly = 1.5 * second + mul(split(r), split(r - 1.5 * second))
    inverse = mul(first_s, split(poly))
    once = jnp.sum(inverse * proj, axis=0, keepdims=True)
    twice = jnp.sum(inverse * once, axis=1, keepdims=True) * (1.0 / scale)
    wmean = jnp.sum(jnp.where(diag, twice, 0.0), axis=0, keepdims=True)
    full = jnp.sqrt((MEMBERS - 1.0) / scale) * inverse + wmean
    return full - jnp.mean(full, axis=1, keepdims=True) + 1.0 / MEMBERS


def kernel(
    st_hbm, ob_hbm, val_hbm, prec_hbm, itab_hbm, ftab_hbm,
    out_ref,
    st_in, st_t, ob_in, ob_t, obs, xbuf, obuf, vals, precs, itab, ftab, itab_s, ftab_s,
    vh, vl, local_sem, tab_send, tab_recv, aux_send, aux_recv, ob_send, ob_recv, pair_send, st_send, st_recv, out_send, out_recv,
):
    m = lax.axis_index("mem")
    i = lax.axis_index("tile")
    q = lax.rem(i, 2)
    z = i // 2
    g = 16 * z + m
    sib = (m, i + 1 - 2 * q)
    src_shard = g // 8
    home = src_shard == i

    load_ob = pltpu.make_async_copy(ob_hbm, ob_in, local_sem.at[0])
    load_st = pltpu.make_async_copy(st_hbm, st_in, local_sem.at[1])
    load_ob.start()
    load_st.start()

    barrier = pltpu.get_barrier_semaphore()

    def greet(device):
        pl.semaphore_signal(barrier, inc=1, device_id=device, device_id_type=MESH)

    def greet_source(j, c):
        @pl.when(jnp.logical_not(home & (j == m)))
        def _():
            greet((j, src_shard))
        return c

    def greet_owner(j, c):
        md, td = 8 * q + j // 2, 2 * z + lax.rem(j, 2)

        @pl.when(jnp.logical_not((md == m) & (td == i)))
        def _():
            greet((md, td))
        return c

    def greet_edge(j, c):
        greet((j, lax.rem(src_shard + 2 * q - 1 + 32, 32)))
        return c

    lax.fori_loop(0, 16, greet_source, 0)
    lax.fori_loop(0, 16, greet_owner, 0)
    edge = ((q == 0) & (lax.rem(g, 8) <= 1)) | ((q == 1) & (lax.rem(g, 8) >= 6))

    @pl.when(edge)
    def _():
        lax.fori_loop(0, 16, greet_edge, 0)

    greet(sib)
    greet((m, lax.rem(2 * z + 31, 32)))
    greet((m, lax.rem(2 * z + 2, 32)))

    load_ob.wait()

    def turn_ob(b, c):
        for k in range(4):
            ob_t[4 * b + k] = ob_in[pl.ds(4 * b + k, 16, stride=64), :]
        return c

    lax.fori_loop(0, 16, turn_ob, 0)

    @pl.when(home)
    def _():
        pl.semaphore_wait(barrier, 37)

    @pl.when(jnp.logical_not(home))
    def _():
        pl.semaphore_wait(barrier, 39)

    def remote(src, dst, ss, rs, device):
        return pltpu.make_async_remote_copy(src_ref=src, dst_ref=dst, send_sem=ss, recv_sem=rs, device_id=device, device_id_type=MESH)

    own_itab = pltpu.make_async_copy(itab_hbm, itab.at[0], local_sem.at[2])
    own_ftab = pltpu.make_async_copy(ftab_hbm, ftab.at[0], local_sem.at[3])
    own_itab.start()
    own_ftab.start()
    tabs = [
        remote(itab_hbm, itab.at[1], tab_send.at[0], tab_recv.at[0], sib),
        remote(ftab_hbm, ftab.at[1], tab_send.at[1], tab_recv.at[1], sib),
    ]
    far = 2 * lax.rem(z + 2 * q - 1 + 16, 16)
    auxes = []
    owns = []
    for n, (hbm, buf) in enumerate(((val_hbm, vals), (prec_hbm, precs))):
        owns.append(pltpu.make_async_copy(hbm, buf.at[q + 1], aux_recv.at[n, q + 1]))
        auxes.append(remote(hbm, buf.at[q + 1], aux_send.at[n, 0], aux_recv.at[n, q + 1], sib))
        for core in range(2):
            auxes.append(remote(hbm, buf.at[3 - 3 * q], aux_send.at[n, 1 + core], aux_recv.at[n, 3 - 3 * q], (m, far + core)))
    for copy in tabs + owns + auxes:
        copy.start()

    def ob_unit(w, k):
        kk = lax.rem(k + m, 8)
        gd = lax.rem(8 * i + kk + 2 - w // 2 + 256, 256)
        md, td = lax.rem(gd, 16), 2 * (gd // 16) + w // 5
        src = ob_t.at[pl.ds(4 * (2 * kk + w % 2), 4)]
        dst = obs.at[pl.ds(4 * (w - w // 5), 4), pl.ds(pl.multiple_of(16 * m, 16), 16)]
        away = remote(src, dst, ob_send.at[w, k], ob_recv.at[w], (md, td))
        stay = pltpu.make_async_copy(src, dst, ob_recv.at[w])
        return (md == m) & (td == i), away, stay

    order = (1, 5, 2, 6, 3, 7, 4, 8, 0, 9)
    for w in order:
        def send_ob(k, c):
            here, away, stay = ob_unit(w, k)

            @pl.when(here)
            def _():
                stay.start()

            @pl.when(jnp.logical_not(here))
            def _():
                away.start()
            return c

        lax.fori_loop(0, 8, send_ob, 0)

    load_st.wait()

    def turn_st(b, c):
        for k in range(8):
            st_t[8 * b + k] = st_in[pl.ds(8 * b + k, 16, stride=256), :]
        return c

    lax.fori_loop(0, 32, turn_st, 0)

    def st_unit(t, j):
        kk, core = lax.rem(j // 2 + m, 8), lax.rem(j, 2)
        md, td = 8 * q + kk, 2 * z + core
        src = st_t.at[pl.ds(16 * (2 * kk + core) + 4 * t, 4)]
        dst = xbuf.at[pl.ds(4 * t, 4), pl.ds(pl.multiple_of(16 * m, 16), 16)]
        away = remote(src, dst, st_send.at[t, j], st_recv.at[t], (md, td))
        stay = pltpu.make_async_copy(src, dst, st_recv.at[t])
        return (md == m) & (td == i), away, stay

    for t in range(PER):
        def send_st(j, c):
            here, away, stay = st_unit(t, j)

            @pl.when(here)
            def _():
                stay.start()

            @pl.when(jnp.logical_not(here))
            def _():
                away.start()
            return c

        lax.fori_loop(0, 16, send_st, 0)

    own_itab.wait()
    own_ftab.wait()
    for copy in tabs:
        copy.wait_recv()
    which = jnp.where(home, 0, 1)
    to_smem = [
        pltpu.make_async_copy(itab.at[which], itab_s, local_sem.at[4]),
        pltpu.make_async_copy(ftab.at[which], ftab_s, local_sem.at[5]),
    ]
    for copy in to_smem:
        copy.start()
    for copy in to_smem:
        copy.wait()
    for n, (hbm, buf) in enumerate(((val_hbm, vals), (prec_hbm, precs))):
        for slot in range(4):
            pltpu.make_async_copy(hbm, buf.at[slot], aux_recv.at[n, slot]).wait()

    def ob_block(w, slot):
        ref = obs.at[pl.ds(4 * slot, 4)]
        return pltpu.make_async_copy(ref, ref, ob_recv.at[w])

    pairs = []
    for e in range(4):
        w = 1 + 4 * q + e
        ob_block(w, w - q).wait()
        copy = remote(obs.at[pl.ds(4 * (w - q), 4)], obs.at[pl.ds(4 * (w - 1 + q), 4)], pair_send.at[e], ob_recv.at[w], sib)
        copy.start()
        pairs.append(copy)
    ob_block(9 * q, 8 * q).wait()
    for e in range(4):
        w = 5 - 4 * q + e
        ob_block(w, w - q).wait()

    def tile_step(t, c):
        row = 8 * lax.rem(g, 8) + 4 * q + t
        line, base = row // 8, 16 * lax.rem(row, 8)
        count = itab_s[line, base + SLOTS]
        proj = jnp.zeros((MEMBERS, 128), F32)
        for s in range(SLOTS):
            batch = itab_s[line, base + s]
            place = lax.rem(batch - (8 * g - 16 + 4 * q) + 4096, 2048)
            place = jnp.clip(place, 0, WINDOW - 1)
            where = lax.rem(batch - (128 * z - 64) + 4096, 2048)
            where = jnp.clip(where, 0, 255)
            shard, line_b = where // 64, lax.rem(where, 64)
            prior = obs[place]
            value = vals[shard, pl.ds(line_b, 1), :]
            prec = precs[shard, pl.ds(line_b, 1), :]
            weight = jnp.where(s < count, ftab_s[line, base + s], 0.0)
            size = jnp.sqrt(prec * weight)
            ymean = jnp.mean(prior, axis=0, keepdims=True)
            scaled = (prior - ymean) * size
            proj = proj + scaled * ((value - ymean) * size)
            high, low = split(scaled)
            vh[:, 128 * s : 128 * (s + 1)] = high
            vl[:, 128 * s : 128 * (s + 1)] = low
        both = (vh[...], vl[...])
        gram = mul(both, both, NT)
        turn = transform(gram, jnp.sum(proj, axis=1, keepdims=True))
        turn_s = split(turn)

        whole = xbuf.at[pl.ds(4 * t, 4)]
        pltpu.make_async_copy(whole, whole, st_recv.at[t]).wait()
        for half in range(2):
            x = jnp.concatenate([xbuf[4 * t + 2 * half], xbuf[4 * t + 2 * half + 1]], axis=1)
            moved = mul(turn_s, split(x))
            obuf[4 * t + 2 * half] = moved[:, :128]
            obuf[4 * t + 2 * half + 1] = moved[:, 128:]

        def send_out(j, c):
            md = lax.rem(j + m, 16)
            here, away, stay = out_unit(t, j)

            @pl.when(here)
            def _():
                stay.start()

            @pl.when(jnp.logical_not(here))
            def _():
                away.start()
            return c

        lax.fori_loop(0, 16, send_out, 0)
        return c

    def out_unit(t, j):
        md = lax.rem(j + m, 16)
        row = 4 * (8 * lax.rem(g, 8) + 4 * q + t)
        src = obuf.at[pl.ds(4 * t, 4), pl.ds(pl.multiple_of(16 * md, 16), 16)]
        dst = out_ref.at[pl.ds(row, 4)]
        away = remote(src, dst, out_send.at[t, j], out_recv.at[0], (md, src_shard))
        stay = pltpu.make_async_copy(src, dst, out_recv.at[0])
        return (md == m) & home, away, stay

    lax.fori_loop(0, PER, tile_step, 0)

    for copy in tabs + auxes:
        copy.wait_send()
    for copy in pairs:
        copy.wait_send()
    for w in range(10):
        def left_ob(k, c):
            here, away, stay = ob_unit(w, k)

            @pl.when(jnp.logical_not(here))
            def _():
                away.wait_send()
            return c

        lax.fori_loop(0, 8, left_ob, 0)

    def left_t(t, c):
        def left_j(j, c):
            here, away, stay = st_unit(t, j)

            @pl.when(jnp.logical_not(here))
            def _():
                away.wait_send()
            here, away, stay = out_unit(t, j)

            @pl.when(jnp.logical_not(here))
            def _():
                away.wait_send()
            return c

        return lax.fori_loop(0, 16, left_j, c)

    lax.fori_loop(0, PER, left_t, 0)
    pltpu.make_async_copy(out_ref, out_ref, out_recv.at[0]).wait()


def per_device(state, obs_prior, obs_value, obs_prec, tile_batches, tile_count, loc_weight):
    itab = jnp.concatenate([tile_batches, tile_count[:, None], jnp.zeros((64, 9), jnp.int32)], axis=1).reshape(8, 128)
    ftab = jnp.concatenate([loc_weight, jnp.zeros((64, 10), F32)], axis=1).reshape(8, 128)
    anywhere = pl.BlockSpec(memory_space=pl.ANY)
    dma = pltpu.SemaphoreType.DMA
    out = pl.pallas_call(
        kernel,
        out_shape=jax.ShapeDtypeStruct((256, 16, 128), F32),
        in_specs=[anywhere] * 6,
        out_specs=anywhere,
        scratch_shapes=[
            pltpu.VMEM((16 * 256, 128), F32),
            pltpu.VMEM((256, 16, 128), F32),
            pltpu.VMEM((16 * 64, 128), F32),
            pltpu.VMEM((64, 16, 128), F32),
            pltpu.VMEM((WINDOW, MEMBERS, 128), F32),
            pltpu.VMEM((16, MEMBERS, 128), F32),
            pltpu.VMEM((16, MEMBERS, 128), F32),
            pltpu.VMEM((4, 64, 128), F32),
            pltpu.VMEM((4, 64, 128), F32),
            pltpu.VMEM((2, 8, 128), jnp.int32),
            pltpu.VMEM((2, 8, 128), F32),
            pltpu.SMEM((8, 128), jnp.int32),
            pltpu.SMEM((8, 128), F32),
            pltpu.VMEM((MEMBERS, SLOTS * 128), BF16),
            pltpu.VMEM((MEMBERS, SLOTS * 128), BF16),
            dma((6,)),
            dma((2,)),
            dma((2,)),
            dma((2, 3)),
            dma((2, 4)),
            dma((10, 8)),
            dma((10,)),
            dma((4,)),
            dma((4, 16)),
            dma((4,)),
            dma((4, 16)),
            dma((1,)),
        ],
        compiler_params=pltpu.CompilerParams(collective_id=0, has_side_effects=True, vmem_limit_bytes=48 * 2**20),
        name="etkf",
    )(
        state.reshape(16 * 256, 128),
        obs_prior.reshape(16 * 64, 128),
        obs_value,
        obs_prec,
        itab,
        ftab,
    )
    return jnp.transpose(out, (1, 0, 2)).reshape(16, 64, 4, 128)


def solution(mesh):
    in_specs = (
        P("mem", "tile", None, None),
        P("mem", "tile", None),
        P("tile", None),
        P("tile", None),
        P("tile", None),
        P("tile"),
        P("tile", None),
    )
    out_specs = P("mem", "tile", None, None)
    return jax.shard_map(
        per_device, mesh=mesh, in_specs=in_specs, out_specs=out_specs, check_vma=False
    )
```

```python
import jax
import jax.numpy as jnp
from jax import lax
from jax.experimental import pallas as pl
from jax.experimental.pallas import tpu as pltpu
from jax.sharding import PartitionSpec as P

MESH = pl.DeviceIdType.MESH
MEMBERS = 256
SLOTS = 6
PER = 4
WINDOW = 36
STEP = 1
OSTEP = 1
GROUPS = ((0, 2), (2, 2), (4, 1), (5, 1), (6, 2), (8, 2))
ORDER = (2, 3, 1, 4, 0, 5)

F32 = jnp.float32
BF16 = jnp.bfloat16
NN = (((1,), (0,)), ((), ()))
NT = (((1,), (1,)), ((), ()))


def split(x):
    high = x.astype(BF16)
    return high, (x - high.astype(F32)).astype(BF16)


def mxu(a, b, dims=NN):
    return lax.dot_general(a, b, dims, preferred_element_type=F32)


def mul(a, b, dims=NN):
    ah, al = a
    bh, bl = b
    return mxu(ah, bh, dims) + (mxu(ah, bl, dims) + mxu(al, bh, dims))


def transform(gram, proj):
    rows = lax.broadcasted_iota(jnp.int32, (MEMBERS, MEMBERS), 0)
    cols = lax.broadcasted_iota(jnp.int32, (MEMBERS, MEMBERS), 1)
    diag = rows == cols
    ident = diag.astype(F32)
    amat = (MEMBERS - 1.0) * ident + gram
    scale = jnp.sqrt(jnp.sum(amat * amat, keepdims=True))
    root = amat * (1.0 / scale)
    first = 1.5 * ident - 0.5 * root
    root_s = split(root)
    first_s = split(first)
    square = mul(root_s, root_s)
    inner = mul(first_s, split(1.5 * root - 0.5 * square))
    second = 1.5 * ident - 0.5 * inner
    second_s = split(second)
    r = mul(second_s, second_s)
    poly = 1.5 * second + mul(split(r), split(r - 1.5 * second))
    inverse = mul(first_s, split(poly))
    once = jnp.sum(inverse * proj, axis=0, keepdims=True)
    twice = jnp.sum(inverse * once, axis=1, keepdims=True) * (1.0 / scale)
    wmean = jnp.sum(jnp.where(diag, twice, 0.0), axis=0, keepdims=True)
    full = jnp.sqrt((MEMBERS - 1.0) / scale) * inverse + wmean
    return full - jnp.mean(full, axis=1, keepdims=True) + 1.0 / MEMBERS


def kernel(
    st_hbm, ob_hbm, val_hbm, prec_hbm, itab_hbm, ctab_hbm, ftab_hbm,
    out_ref,
    st_in, st_t, ob_in, ob_t, obs, xbuf, obuf, vals, precs, itab, ctab, ftab, itab_s, ctab_s, ftab_s,
    vh, vl, th, tl, local_sem, tab_send, tab_recv, aux_send, aux_recv, ob_send, ob_recv, pair_send, pair_recv, st_send, st_recv, out_send, out_recv,
):
    m = lax.axis_index("mem")
    i = lax.axis_index("tile")
    q = lax.rem(i, 2)
    z = i // 2
    g = 16 * z + m
    sib = (m, i + 1 - 2 * q)
    src_shard = g // 8
    home = src_shard == i

    load_ob = pltpu.make_async_copy(ob_hbm, ob_in, local_sem.at[0])
    load_st = pltpu.make_async_copy(st_hbm, st_in, local_sem.at[1])
    load_ob.start()
    load_st.start()

    barrier = pltpu.get_barrier_semaphore()

    def greet(device):
        pl.semaphore_signal(barrier, inc=1, device_id=device, device_id_type=MESH)

    def greet_source(j, c):
        @pl.when(jnp.logical_not(home & (j == m)))
        def _():
            greet((j, src_shard))
        return c

    def greet_owner(j, c):
        md, td = 8 * q + j // 2, 2 * z + lax.rem(j, 2)

        @pl.when(jnp.logical_not((md == m) & (td == i)))
        def _():
            greet((md, td))
        return c

    def greet_edge(j, c):
        greet((j, lax.rem(src_shard + 2 * q - 1 + 32, 32)))
        return c

    lax.fori_loop(0, 16, greet_source, 0)
    lax.fori_loop(0, 16, greet_owner, 0)
    edge = ((q == 0) & (lax.rem(g, 8) <= 1)) | ((q == 1) & (lax.rem(g, 8) >= 6))

    @pl.when(edge)
    def _():
        lax.fori_loop(0, 16, greet_edge, 0)

    greet(sib)
    greet((m, lax.rem(2 * z + 31, 32)))
    greet((m, lax.rem(2 * z + 2, 32)))

    load_ob.wait()

    def turn_ob(b, c):
        for k in range(4):
            ob_t[4 * b + k] = ob_in[pl.ds(4 * b + k, 16, stride=64), :]
        return c

    lax.fori_loop(0, 16, turn_ob, 0)

    @pl.when(home)
    def _():
        pl.semaphore_wait(barrier, 37)

    @pl.when(jnp.logical_not(home))
    def _():
        pl.semaphore_wait(barrier, 39)

    def remote(src, dst, ss, rs, device):
        return pltpu.make_async_remote_copy(src_ref=src, dst_ref=dst, send_sem=ss, recv_sem=rs, device_id=device, device_id_type=MESH)

    tables = ((itab_hbm, itab, itab_s), (ctab_hbm, ctab, ctab_s), (ftab_hbm, ftab, ftab_s))
    own_tabs, tabs = [], []
    for n, (hbm, buf, smem) in enumerate(tables):
        own_tabs.append(pltpu.make_async_copy(hbm, buf.at[0], local_sem.at[2 + n]))
        tabs.append(remote(hbm, buf.at[1], tab_send.at[n], tab_recv.at[n], sib))
    far = 2 * lax.rem(z + 2 * q - 1 + 16, 16)
    auxes = []
    owns = []
    for n, (hbm, buf) in enumerate(((val_hbm, vals), (prec_hbm, precs))):
        owns.append(pltpu.make_async_copy(hbm, buf.at[q + 1], aux_recv.at[n, q + 1]))
        auxes.append(remote(hbm, buf.at[q + 1], aux_send.at[n, 0], aux_recv.at[n, q + 1], sib))
        for core in range(2):
            auxes.append(remote(hbm, buf.at[3 - 3 * q], aux_send.at[n, 1 + core], aux_recv.at[n, 3 - 3 * q], (m, far + core)))
    for copy in own_tabs + tabs + owns + auxes:
        copy.start()

    def ob_group(n, k):
        w, size = GROUPS[n]
        core = w // 5
        kk = lax.rem(k + m, 8)
        gd = lax.rem(8 * i + kk + 2 - w // 2 + 256, 256)
        md, td = lax.rem(gd, 16), 2 * (gd // 16) + core
        src = ob_t.at[pl.ds(4 * (2 * kk + w % 2), 4 * size)]
        dst = obs.at[pl.ds(4 * (w - core), 4 * size), pl.ds(pl.multiple_of(16 * m, 16), 16)]

        def away():
            return remote(src, dst, ob_send.at[n, k], ob_recv.at[n], (md, td))

        def stay():
            return pltpu.make_async_copy(src, dst, ob_recv.at[n])

        return (md == m) & (td == i), away, stay

    def launch(unit):
        here, away, stay = unit

        @pl.when(here)
        def _():
            stay().start()

        @pl.when(jnp.logical_not(here))
        def _():
            away().start()

    def left(unit):
        here, away, stay = unit

        @pl.when(jnp.logical_not(here))
        def _():
            away().wait_send()

    def each(count, act):
        def body(j, c):
            act(j)
            return c

        lax.fori_loop(0, count, body, 0)

    for n in ORDER:
        each(8, lambda k: launch(ob_group(n, k)))

    load_st.wait()

    def turn_st(b, c):
        for k in range(8):
            st_t[8 * b + k] = st_in[pl.ds(8 * b + k, 16, stride=256), :]
        return c

    lax.fori_loop(0, 32, turn_st, 0)

    def st_unit(t, j):
        kk, core = lax.rem(j // 2 + m, 8), lax.rem(j, 2)
        md, td = 8 * q + kk, 2 * z + core
        src = st_t.at[pl.ds(16 * (2 * kk + core) + 4 * STEP * t, 4 * STEP)]
        dst = xbuf.at[pl.ds(4 * STEP * t, 4 * STEP), pl.ds(pl.multiple_of(16 * m, 16), 16)]

        def away():
            return remote(src, dst, st_send.at[t, j], st_recv.at[t], (md, td))

        def stay():
            return pltpu.make_async_copy(src, dst, st_recv.at[t])

        return (md == m) & (td == i), away, stay

    for t in range(PER // STEP):
        each(16, lambda j: launch(st_unit(t, j)))

    for copy in own_tabs:
        copy.wait()
    for copy in tabs:
        copy.wait_recv()
    which = jnp.where(home, 0, 1)
    to_smem = []
    for n, (hbm, buf, smem) in enumerate(tables):
        to_smem.append(pltpu.make_async_copy(buf.at[which], smem, local_sem.at[5 + n]))
    for copy in to_smem:
        copy.start()
    for copy in to_smem:
        copy.wait()
    for n, (hbm, buf) in enumerate(((val_hbm, vals), (prec_hbm, precs))):
        for slot in range(4):
            pltpu.make_async_copy(hbm, buf.at[slot], aux_recv.at[n, slot]).wait()

    def landed(slot, size, sem):
        ref = obs.at[pl.ds(slot, size)]
        pltpu.make_async_copy(ref, ref, sem).wait()

    landed(16 * q, 8, ob_recv.at[5 * q])
    landed(8 + 16 * q, 8, ob_recv.at[1 + 3 * q])
    landed(16, 4, ob_recv.at[2 + q])
    pair = remote(obs.at[pl.ds(4 + 12 * q, 16)], obs.at[pl.ds(20 * q, 16)], pair_send.at[0], pair_recv.at[0], sib)
    pair.start()
    landed(20 - 20 * q, 16, pair_recv.at[0])

    def tile_step(t, c):
        row = 8 * lax.rem(g, 8) + 4 * q + t
        count = ctab_s[0, row]
        proj = jnp.zeros((MEMBERS, 128), F32)
        for s in range(SLOTS):
            batch = itab_s[s, row]
            place = lax.rem(batch - (8 * g - 16 + 4 * q) + 4096, 2048)
            place = jnp.clip(place, 0, WINDOW - 1)
            where = lax.rem(batch - (128 * z - 64) + 4096, 2048)
            where = jnp.clip(where, 0, 255)
            shard, line_b = where // 64, lax.rem(where, 64)
            prior = obs[place]
            value = vals[shard, pl.ds(line_b, 1), :]
            prec = precs[shard, pl.ds(line_b, 1), :]
            weight = jnp.where(s < count, ftab_s[s, row], 0.0)
            size = jnp.sqrt(prec * weight)
            ymean = jnp.mean(prior, axis=0, keepdims=True)
            scaled = (prior - ymean) * size
            proj = proj + scaled * ((value - ymean) * size)
            high, low = split(scaled)
            vh[:, 128 * s : 128 * (s + 1)] = high
            vl[:, 128 * s : 128 * (s + 1)] = low
        both = (vh[...], vl[...])
        gram = mul(both, both, NT)
        turn = transform(gram, jnp.sum(proj, axis=1, keepdims=True))
        high, low = split(turn)
        th[t] = high
        tl[t] = low
        return c

    def apply_step(t, c):
        turn_s = (th[t], tl[t])

        @pl.when(lax.rem(t, STEP) == 0)
        def _():
            whole = xbuf.at[pl.ds(4 * t, 4 * STEP)]
            pltpu.make_async_copy(whole, whole, st_recv.at[t // STEP]).wait()

        for half in range(2):
            x = jnp.concatenate([xbuf[4 * t + 2 * half], xbuf[4 * t + 2 * half + 1]], axis=1)
            moved = mul(turn_s, split(x))
            obuf[4 * t + 2 * half] = moved[:, :128]
            obuf[4 * t + 2 * half + 1] = moved[:, 128:]

        @pl.when(lax.rem(t, OSTEP) == OSTEP - 1)
        def _():
            each(16, lambda j: launch(out_unit(t // OSTEP, j)))

        return c

    def out_unit(t, j):
        md = lax.rem(j + m, 16)
        row = 4 * (8 * lax.rem(g, 8) + 4 * q + OSTEP * t)
        src = obuf.at[pl.ds(4 * OSTEP * t, 4 * OSTEP), pl.ds(pl.multiple_of(16 * md, 16), 16)]
        dst = out_ref.at[pl.ds(row, 4 * OSTEP)]

        def away():
            return remote(src, dst, out_send.at[t, j], out_recv.at[0], (md, src_shard))

        def stay():
            return pltpu.make_async_copy(src, dst, out_recv.at[0])

        return (md == m) & home, away, stay

    lax.fori_loop(0, PER, tile_step, 0)
    lax.fori_loop(0, PER, apply_step, 0)

    for copy in tabs + auxes:
        copy.wait_send()
    pair.wait_send()
    for n in range(len(GROUPS)):
        each(8, lambda k: left(ob_group(n, k)))
    for t in range(PER // STEP):
        each(16, lambda j: left(st_unit(t, j)))
    for t in range(PER // OSTEP):
        each(16, lambda j: left(out_unit(t, j)))
    pltpu.make_async_copy(out_ref, out_ref, out_recv.at[0]).wait()


def per_device(state, obs_prior, obs_value, obs_prec, tile_batches, tile_count, loc_weight):
    anywhere = pl.BlockSpec(memory_space=pl.ANY)
    dma = pltpu.SemaphoreType.DMA
    out = pl.pallas_call(
        kernel,
        out_shape=jax.ShapeDtypeStruct((256, 16, 128), F32),
        in_specs=[anywhere] * 7,
        out_specs=anywhere,
        scratch_shapes=[
            pltpu.VMEM((16 * 256, 128), F32),
            pltpu.VMEM((256, 16, 128), F32),
            pltpu.VMEM((16 * 64, 128), F32),
            pltpu.VMEM((64, 16, 128), F32),
            pltpu.VMEM((WINDOW, MEMBERS, 128), F32),
            pltpu.VMEM((16, MEMBERS, 128), F32),
            pltpu.VMEM((16, MEMBERS, 128), F32),
            pltpu.VMEM((4, 64, 128), F32),
            pltpu.VMEM((4, 64, 128), F32),
            pltpu.VMEM((2, SLOTS, 64), jnp.int32),
            pltpu.VMEM((2, 1, 64), jnp.int32),
            pltpu.VMEM((2, SLOTS, 64), F32),
            pltpu.SMEM((SLOTS, 64), jnp.int32),
            pltpu.SMEM((1, 64), jnp.int32),
            pltpu.SMEM((SLOTS, 64), F32),
            pltpu.VMEM((MEMBERS, SLOTS * 128), BF16),
            pltpu.VMEM((MEMBERS, SLOTS * 128), BF16),
            pltpu.VMEM((PER, MEMBERS, MEMBERS), BF16),
            pltpu.VMEM((PER, MEMBERS, MEMBERS), BF16),
            dma((8,)),
            dma((3,)),
            dma((3,)),
            dma((2, 3)),
            dma((2, 4)),
            dma((6, 8)),
            dma((6,)),
            dma((1,)),
            dma((1,)),
            dma((4, 16)),
            dma((4,)),
            dma((4, 16)),
            dma((1,)),
        ],
        compiler_params=pltpu.CompilerParams(collective_id=0, has_side_effects=True, vmem_limit_bytes=60 * 2**20),
        name="etkf",
    )(
        state.reshape(16 * 256, 128),
        obs_prior.reshape(16 * 64, 128),
        obs_value,
        obs_prec,
        tile_batches.T,
        tile_count.reshape(1, 64),
        loc_weight.T,
    )
    return jnp.transpose(out, (1, 0, 2)).reshape(16, 64, 4, 128)


def solution(mesh):
    in_specs = (
        P("mem", "tile", None, None),
        P("mem", "tile", None),
        P("tile", None),
        P("tile", None),
        P("tile", None),
        P("tile"),
        P("tile", None),
    )
    out_specs = P("mem", "tile", None, None)
    return jax.shard_map(
        per_device, mesh=mesh, in_specs=in_specs, out_specs=out_specs, check_vma=False
    )
```

```python
import jax
import jax.numpy as jnp
from jax import lax
from jax.experimental import pallas as pl
from jax.experimental.pallas import tpu as pltpu
from jax.sharding import PartitionSpec as P

MESH = pl.DeviceIdType.MESH
MEMBERS = 256
SLOTS = 6
PER = 4
WINDOW = 36
STEP = 1
OSTEP = 1
TURNS = 2
GROUPS = ((0, 2), (2, 2), (4, 1), (5, 1), (6, 2), (8, 2))
ORDER = (2, 3, 1, 4, 0, 5)

F32 = jnp.float32
BF16 = jnp.bfloat16
NN = (((1,), (0,)), ((), ()))
NT = (((1,), (1,)), ((), ()))


def split(x):
    high = x.astype(BF16)
    return high, (x - high.astype(F32)).astype(BF16)


def mxu(a, b, dims=NN):
    return lax.dot_general(a, b, dims, preferred_element_type=F32)


def mul(a, b, dims=NN):
    ah, al = a
    bh, bl = b
    return mxu(ah, bh, dims) + (mxu(ah, bl, dims) + mxu(al, bh, dims))


def transform(gram, proj):
    rows = lax.broadcasted_iota(jnp.int32, (MEMBERS, MEMBERS), 0)
    cols = lax.broadcasted_iota(jnp.int32, (MEMBERS, MEMBERS), 1)
    diag = rows == cols
    ident = diag.astype(F32)
    amat = (MEMBERS - 1.0) * ident + gram
    scale = jnp.sqrt(jnp.sum(amat * amat, keepdims=True))
    root = amat * (1.0 / scale)
    first = 1.5 * ident - 0.5 * root
    root_s = split(root)
    first_s = split(first)
    square = mul(root_s, root_s)
    inner = mul(first_s, split(1.5 * root - 0.5 * square))
    second = 1.5 * ident - 0.5 * inner
    second_s = split(second)
    r = mul(second_s, second_s)
    poly = 1.5 * second + mul(split(r), split(r - 1.5 * second))
    inverse = mul(first_s, split(poly))
    once = jnp.sum(inverse * proj, axis=0, keepdims=True)
    twice = jnp.sum(inverse * once, axis=1, keepdims=True) * (1.0 / scale)
    wmean = jnp.sum(jnp.where(diag, twice, 0.0), axis=0, keepdims=True)
    full = jnp.sqrt((MEMBERS - 1.0) / scale) * inverse + wmean
    return full - jnp.mean(full, axis=1, keepdims=True) + 1.0 / MEMBERS


def kernel(
    st_hbm, ob_hbm, val_hbm, prec_hbm, itab_hbm, ctab_hbm, ftab_hbm,
    out_ref,
    st_in, st_t, ob_in, ob_t, obs, xbuf, obuf, vals, precs, itab, ctab, ftab, itab_s, ctab_s, ftab_s,
    vh, vl, th, tl, local_sem, tab_send, tab_recv, aux_send, aux_recv, ob_send, ob_recv, pair_send, pair_recv, st_send, st_recv, out_send, out_recv,
):
    m = lax.axis_index("mem")
    i = lax.axis_index("tile")
    q = lax.rem(i, 2)
    z = i // 2
    g = 16 * z + m
    sib = (m, i + 1 - 2 * q)
    src_shard = g // 8
    home = src_shard == i

    load_ob = pltpu.make_async_copy(ob_hbm, ob_in, local_sem.at[0])
    load_st = pltpu.make_async_copy(st_hbm, st_in, local_sem.at[1])
    load_ob.start()
    load_st.start()

    barrier = pltpu.get_barrier_semaphore()

    def greet(device):
        pl.semaphore_signal(barrier, inc=1, device_id=device, device_id_type=MESH)

    def greet_source(j, c):
        @pl.when(jnp.logical_not(home & (j == m)))
        def _():
            greet((j, src_shard))
        return c

    def greet_owner(j, c):
        md, td = 8 * q + j // 2, 2 * z + lax.rem(j, 2)

        @pl.when(jnp.logical_not((md == m) & (td == i)))
        def _():
            greet((md, td))
        return c

    def greet_edge(j, c):
        greet((j, lax.rem(src_shard + 2 * q - 1 + 32, 32)))
        return c

    lax.fori_loop(0, 16, greet_source, 0)
    lax.fori_loop(0, 16, greet_owner, 0)
    edge = ((q == 0) & (lax.rem(g, 8) <= 1)) | ((q == 1) & (lax.rem(g, 8) >= 6))

    @pl.when(edge)
    def _():
        lax.fori_loop(0, 16, greet_edge, 0)

    greet(sib)
    greet((m, lax.rem(2 * z + 31, 32)))
    greet((m, lax.rem(2 * z + 2, 32)))

    load_ob.wait()

    def turn_ob(b, c):
        for k in range(4):
            ob_t[4 * b + k] = ob_in[pl.ds(4 * b + k, 16, stride=64), :]
        return c

    lax.fori_loop(0, 16, turn_ob, 0)

    @pl.when(home)
    def _():
        pl.semaphore_wait(barrier, 37)

    @pl.when(jnp.logical_not(home))
    def _():
        pl.semaphore_wait(barrier, 39)

    def remote(src, dst, ss, rs, device):
        return pltpu.make_async_remote_copy(src_ref=src, dst_ref=dst, send_sem=ss, recv_sem=rs, device_id=device, device_id_type=MESH)

    tables = ((itab_hbm, itab, itab_s), (ctab_hbm, ctab, ctab_s), (ftab_hbm, ftab, ftab_s))
    own_tabs, tabs = [], []
    for n, (hbm, buf, smem) in enumerate(tables):
        own_tabs.append(pltpu.make_async_copy(hbm, buf.at[0], local_sem.at[2 + n]))
        tabs.append(remote(hbm, buf.at[1], tab_send.at[n], tab_recv.at[n], sib))
    far = 2 * lax.rem(z + 2 * q - 1 + 16, 16)
    auxes = []
    owns = []
    for n, (hbm, buf) in enumerate(((val_hbm, vals), (prec_hbm, precs))):
        owns.append(pltpu.make_async_copy(hbm, buf.at[q + 1], aux_recv.at[n, q + 1]))
        auxes.append(remote(hbm, buf.at[q + 1], aux_send.at[n, 0], aux_recv.at[n, q + 1], sib))
        for core in range(2):
            auxes.append(remote(hbm, buf.at[3 - 3 * q], aux_send.at[n, 1 + core], aux_recv.at[n, 3 - 3 * q], (m, far + core)))

    def ob_group(n, k):
        w, size = GROUPS[n]
        core = w // 5
        kk = lax.rem(k + m + 2, 8)
        gd = lax.rem(8 * i + kk + 2 - w // 2 + 256, 256)
        md, td = lax.rem(gd, 16), 2 * (gd // 16) + core
        src = ob_t.at[pl.ds(4 * (2 * kk + w % 2), 4 * size)]
        dst = obs.at[pl.ds(4 * (w - core), 4 * size), pl.ds(pl.multiple_of(16 * m, 16), 16)]

        def away():
            return remote(src, dst, ob_send.at[n, k], ob_recv.at[n], (md, td))

        def stay():
            return pltpu.make_async_copy(src, dst, ob_recv.at[n])

        return (md == m) & (td == i), away, stay

    def launch(unit):
        here, away, stay = unit

        @pl.when(here)
        def _():
            stay().start()

        @pl.when(jnp.logical_not(here))
        def _():
            away().start()

    def left(unit):
        here, away, stay = unit

        @pl.when(jnp.logical_not(here))
        def _():
            away().wait_send()

    def each(count, act):
        def body(j, c):
            act(j)
            return c

        lax.fori_loop(0, count, body, 0)

    for n in ORDER[:2]:
        each(8, lambda k: launch(ob_group(n, k)))
    for copy in own_tabs + tabs + owns + auxes:
        copy.start()
    for n in ORDER[2:]:
        each(8, lambda k: launch(ob_group(n, k)))

    load_st.wait()

    def turn_st(b, c):
        for k in range(8):
            st_t[8 * b + k] = st_in[pl.ds(8 * b + k, 16, stride=256), :]
        return c

    lax.fori_loop(0, 32, turn_st, 0)

    def st_unit(t, j):
        kk, core = lax.rem(j // 2 + m + 2, 8), lax.rem(j, 2)
        md, td = 8 * q + kk, 2 * z + core
        src = st_t.at[pl.ds(16 * (2 * kk + core) + 4 * STEP * t, 4 * STEP)]
        dst = xbuf.at[pl.ds(4 * STEP * t, 4 * STEP), pl.ds(pl.multiple_of(16 * m, 16), 16)]

        def away():
            return remote(src, dst, st_send.at[t, j], st_recv.at[t], (md, td))

        def stay():
            return pltpu.make_async_copy(src, dst, st_recv.at[t])

        return (md == m) & (td == i), away, stay

    for t in range(PER // STEP):
        each(16, lambda j: launch(st_unit(t, j)))

    for copy in own_tabs:
        copy.wait()
    for copy in tabs:
        copy.wait_recv()
    which = jnp.where(home, 0, 1)
    to_smem = []
    for n, (hbm, buf, smem) in enumerate(tables):
        to_smem.append(pltpu.make_async_copy(buf.at[which], smem, local_sem.at[5 + n]))
    for copy in to_smem:
        copy.start()
    for copy in to_smem:
        copy.wait()
    for n, (hbm, buf) in enumerate(((val_hbm, vals), (prec_hbm, precs))):
        for slot in range(4):
            pltpu.make_async_copy(hbm, buf.at[slot], aux_recv.at[n, slot]).wait()

    def landed(slot, size, sem):
        ref = obs.at[pl.ds(slot, size)]
        pltpu.make_async_copy(ref, ref, sem).wait()

    landed(16 * q, 8, ob_recv.at[5 * q])
    landed(8 + 16 * q, 8, ob_recv.at[1 + 3 * q])
    landed(16, 4, ob_recv.at[2 + q])
    pair = remote(obs.at[pl.ds(4 + 12 * q, 16)], obs.at[pl.ds(20 * q, 16)], pair_send.at[0], pair_recv.at[0], sib)
    pair.start()
    landed(20 - 20 * q, 16, pair_recv.at[0])

    def tile_step(t, c):
        row = 8 * lax.rem(g, 8) + 4 * q + t
        count = ctab_s[0, row]
        proj = jnp.zeros((MEMBERS, 128), F32)
        for s in range(SLOTS):
            batch = itab_s[s, row]
            place = lax.rem(batch - (8 * g - 16 + 4 * q) + 4096, 2048)
            place = jnp.clip(place, 0, WINDOW - 1)
            where = lax.rem(batch - (128 * z - 64) + 4096, 2048)
            where = jnp.clip(where, 0, 255)
            shard, line_b = where // 64, lax.rem(where, 64)
            prior = obs[place]
            value = vals[shard, pl.ds(line_b, 1), :]
            prec = precs[shard, pl.ds(line_b, 1), :]
            weight = jnp.where(s < count, ftab_s[s, row], 0.0)
            size = jnp.sqrt(prec * weight)
            ymean = jnp.mean(prior, axis=0, keepdims=True)
            scaled = (prior - ymean) * size
            proj = proj + scaled * ((value - ymean) * size)
            high, low = split(scaled)
            vh[:, 128 * s : 128 * (s + 1)] = high
            vl[:, 128 * s : 128 * (s + 1)] = low
        both = (vh[...], vl[...])
        gram = mul(both, both, NT)
        turn = transform(gram, jnp.sum(proj, axis=1, keepdims=True))
        high, low = split(turn)
        th[t] = high
        tl[t] = low
        return c

    def apply_step(t, c):
        turn_s = (th[t], tl[t])

        @pl.when(lax.rem(t, STEP) == 0)
        def _():
            whole = xbuf.at[pl.ds(4 * t, 4 * STEP)]
            pltpu.make_async_copy(whole, whole, st_recv.at[t // STEP]).wait()

        for half in range(2):
            x = jnp.concatenate([xbuf[4 * t + 2 * half], xbuf[4 * t + 2 * half + 1]], axis=1)
            moved = mul(turn_s, split(x))
            obuf[4 * t + 2 * half] = moved[:, :128]
            obuf[4 * t + 2 * half + 1] = moved[:, 128:]

        @pl.when(lax.rem(t, OSTEP) == OSTEP - 1)
        def _():
            each(16, lambda j: launch(out_unit(t // OSTEP, j)))

        return c

    def out_unit(t, j):
        md = lax.rem(j + m + 10, 16)
        row = 4 * (8 * lax.rem(g, 8) + 4 * q + OSTEP * t)
        src = obuf.at[pl.ds(4 * OSTEP * t, 4 * OSTEP), pl.ds(pl.multiple_of(16 * md, 16), 16)]
        dst = out_ref.at[pl.ds(row, 4 * OSTEP)]

        def away():
            return remote(src, dst, out_send.at[t, j], out_recv.at[0], (md, src_shard))

        def stay():
            return pltpu.make_async_copy(src, dst, out_recv.at[0])

        return (md == m) & home, away, stay

    lax.fori_loop(0, PER, tile_step, 0)
    lax.fori_loop(0, PER, apply_step, 0)

    for copy in tabs + auxes:
        copy.wait_send()
    pair.wait_send()
    for n in range(len(GROUPS)):
        each(8, lambda k: left(ob_group(n, k)))
    for t in range(PER // STEP):
        each(16, lambda j: left(st_unit(t, j)))
    for t in range(PER // OSTEP):
        each(16, lambda j: left(out_unit(t, j)))
    pltpu.make_async_copy(out_ref, out_ref, out_recv.at[0]).wait()


def turn_kernel(in_ref, out_ref):
    for k in range(16):
        out_ref[k] = in_ref[pl.ds(k, 256 // TURNS, stride=16), :]


def per_device(state, obs_prior, obs_value, obs_prec, tile_batches, tile_count, loc_weight):
    anywhere = pl.BlockSpec(memory_space=pl.ANY)
    dma = pltpu.SemaphoreType.DMA
    out = pl.pallas_call(
        kernel,
        out_shape=jax.ShapeDtypeStruct((256, 16, 128), F32),
        in_specs=[anywhere] * 7,
        out_specs=anywhere,
        scratch_shapes=[
            pltpu.VMEM((16 * 256, 128), F32),
            pltpu.VMEM((256, 16, 128), F32),
            pltpu.VMEM((16 * 64, 128), F32),
            pltpu.VMEM((64, 16, 128), F32),
            pltpu.VMEM((WINDOW, MEMBERS, 128), F32),
            pltpu.VMEM((16, MEMBERS, 128), F32),
            pltpu.VMEM((16, MEMBERS, 128), F32),
            pltpu.VMEM((4, 64, 128), F32),
            pltpu.VMEM((4, 64, 128), F32),
            pltpu.VMEM((2, SLOTS, 64), jnp.int32),
            pltpu.VMEM((2, 1, 64), jnp.int32),
            pltpu.VMEM((2, SLOTS, 64), F32),
            pltpu.SMEM((SLOTS, 64), jnp.int32),
            pltpu.SMEM((1, 64), jnp.int32),
            pltpu.SMEM((SLOTS, 64), F32),
            pltpu.VMEM((MEMBERS, SLOTS * 128), BF16),
            pltpu.VMEM((MEMBERS, SLOTS * 128), BF16),
            pltpu.VMEM((PER, MEMBERS, MEMBERS), BF16),
            pltpu.VMEM((PER, MEMBERS, MEMBERS), BF16),
            dma((8,)),
            dma((3,)),
            dma((3,)),
            dma((2, 3)),
            dma((2, 4)),
            dma((6, 8)),
            dma((6,)),
            dma((1,)),
            dma((1,)),
            dma((4, 16)),
            dma((4,)),
            dma((4, 16)),
            dma((1,)),
        ],
        compiler_params=pltpu.CompilerParams(collective_id=0, has_side_effects=True, vmem_limit_bytes=60 * 2**20),
        name="etkf",
    )(
        state.reshape(16 * 256, 128),
        obs_prior.reshape(16 * 64, 128),
        obs_value,
        obs_prec,
        tile_batches.T,
        tile_count.reshape(1, 64),
        loc_weight.T,
    )
    turned = pl.pallas_call(
        turn_kernel,
        grid=(TURNS,),
        out_shape=jax.ShapeDtypeStruct((16, 256, 128), F32),
        in_specs=[pl.BlockSpec((16 * 256 // TURNS, 128), lambda b: (b, 0))],
        out_specs=pl.BlockSpec((16, 256 // TURNS, 128), lambda b: (0, b, 0)),
        compiler_params=pltpu.CompilerParams(vmem_limit_bytes=60 * 2**20),
        name="turn",
    )(out.reshape(256 * 16, 128))
    return turned.reshape(16, 64, 4, 128)


def solution(mesh):
    in_specs = (
        P("mem", "tile", None, None),
        P("mem", "tile", None),
        P("tile", None),
        P("tile", None),
        P("tile", None),
        P("tile"),
        P("tile", None),
    )
    out_specs = P("mem", "tile", None, None)
    return jax.shard_map(
        per_device, mesh=mesh, in_specs=in_specs, out_specs=out_specs, check_vma=False
    )
```

```python
import jax
import jax.numpy as jnp
from jax import lax
from jax.experimental import pallas as pl
from jax.experimental.pallas import tpu as pltpu
from jax.sharding import PartitionSpec as P

MESH = pl.DeviceIdType.MESH
MEMBERS = 256
SLOTS = 6
PER = 4
WINDOW = 36
STEP = 1
OSTEP = 1
TURNS = 2
GROUPS = ((0, 2), (2, 2), (4, 1), (5, 1), (6, 2), (8, 2))
ORDER = (2, 3, 1, 4, 0, 5)

F32 = jnp.float32
BF16 = jnp.bfloat16
NN = (((1,), (0,)), ((), ()))
NT = (((1,), (1,)), ((), ()))


def split(x):
    high = x.astype(BF16)
    return high, (x - high.astype(F32)).astype(BF16)


def mxu(a, b, dims=NN):
    return lax.dot_general(a, b, dims, preferred_element_type=F32)


def mul(a, b, dims=NN):
    ah, al = a
    bh, bl = b
    return mxu(ah, bh, dims) + (mxu(ah, bl, dims) + mxu(al, bh, dims))


def transform(gram, proj):
    rows = lax.broadcasted_iota(jnp.int32, (MEMBERS, MEMBERS), 0)
    cols = lax.broadcasted_iota(jnp.int32, (MEMBERS, MEMBERS), 1)
    diag = rows == cols
    ident = diag.astype(F32)
    amat = (MEMBERS - 1.0) * ident + gram
    scale = jnp.sqrt(jnp.sum(amat * amat, keepdims=True))
    root = amat * (1.0 / scale)
    first = 1.5 * ident - 0.5 * root
    root_s = split(root)
    first_s = split(first)
    square = mul(root_s, root_s)
    inner = mul(first_s, split(1.5 * root - 0.5 * square))
    second = 1.5 * ident - 0.5 * inner
    second_s = split(second)
    r = mul(second_s, second_s)
    poly = 1.5 * second + mul(split(r), split(r - 1.5 * second))
    inverse = mul(first_s, split(poly))
    once = jnp.sum(inverse * proj, axis=0, keepdims=True)
    twice = jnp.sum(inverse * once, axis=1, keepdims=True) * (1.0 / scale)
    wmean = jnp.sum(jnp.where(diag, twice, 0.0), axis=0, keepdims=True)
    full = jnp.sqrt((MEMBERS - 1.0) / scale) * inverse + wmean
    return full - jnp.mean(full, axis=1, keepdims=True) + 1.0 / MEMBERS


def kernel(
    st_hbm, ob_hbm, val_hbm, prec_hbm, itab_hbm, ctab_hbm, ftab_hbm,
    out_ref,
    st_in, st_t, ob_in, ob_t, obs, xbuf, obuf, vals, precs, itab, ctab, ftab, itab_s, ctab_s, ftab_s,
    vh, vl, th, tl, local_sem, tab_send, tab_recv, aux_send, aux_recv, ob_send, ob_recv, pair_send, pair_recv, st_send, st_recv, out_send, out_recv,
):
    m = lax.axis_index("mem")
    i = lax.axis_index("tile")
    q = lax.rem(i, 2)
    z = i // 2
    g = 16 * z + m
    sib = (m, i + 1 - 2 * q)
    src_shard = g // 8
    home = src_shard == i

    load_ob = pltpu.make_async_copy(ob_hbm, ob_in, local_sem.at[0])
    load_st = pltpu.make_async_copy(st_hbm, st_in, local_sem.at[1])
    load_ob.start()
    load_st.start()

    barrier = pltpu.get_barrier_semaphore()

    def greet(device):
        pl.semaphore_signal(barrier, inc=1, device_id=device, device_id_type=MESH)

    def greet_source(j, c):
        @pl.when(jnp.logical_not(home & (j == m)))
        def _():
            greet((j, src_shard))
        return c

    def greet_owner(j, c):
        md, td = 8 * q + j // 2, 2 * z + lax.rem(j, 2)

        @pl.when(jnp.logical_not((md == m) & (td == i)))
        def _():
            greet((md, td))
        return c

    def greet_edge(j, c):
        greet((j, lax.rem(src_shard + 2 * q - 1 + 32, 32)))
        return c

    lax.fori_loop(0, 16, greet_source, 0)
    lax.fori_loop(0, 16, greet_owner, 0)
    edge = ((q == 0) & (lax.rem(g, 8) <= 1)) | ((q == 1) & (lax.rem(g, 8) >= 6))

    @pl.when(edge)
    def _():
        lax.fori_loop(0, 16, greet_edge, 0)

    greet(sib)
    greet((m, lax.rem(2 * z + 31, 32)))
    greet((m, lax.rem(2 * z + 2, 32)))

    load_ob.wait()

    def turn_ob(b, c):
        for k in range(4):
            ob_t[4 * b + k] = ob_in[pl.ds(4 * b + k, 16, stride=64), :]
        return c

    lax.fori_loop(0, 16, turn_ob, 0)

    @pl.when(home)
    def _():
        pl.semaphore_wait(barrier, 37)

    @pl.when(jnp.logical_not(home))
    def _():
        pl.semaphore_wait(barrier, 39)

    def remote(src, dst, ss, rs, device):
        return pltpu.make_async_remote_copy(src_ref=src, dst_ref=dst, send_sem=ss, recv_sem=rs, device_id=device, device_id_type=MESH)

    tables = ((itab_hbm, itab, itab_s), (ctab_hbm, ctab, ctab_s), (ftab_hbm, ftab, ftab_s))
    own_tabs, tabs = [], []
    for n, (hbm, buf, smem) in enumerate(tables):
        own_tabs.append(pltpu.make_async_copy(hbm, buf.at[0], local_sem.at[2 + n]))
        tabs.append(remote(hbm, buf.at[1], tab_send.at[n], tab_recv.at[n], sib))
    far = 2 * lax.rem(z + 2 * q - 1 + 16, 16)
    auxes = []
    owns = []
    for n, (hbm, buf) in enumerate(((val_hbm, vals), (prec_hbm, precs))):
        owns.append(pltpu.make_async_copy(hbm, buf.at[q + 1], aux_recv.at[n, q + 1]))
        auxes.append(remote(hbm, buf.at[q + 1], aux_send.at[n, 0], aux_recv.at[n, q + 1], sib))
        for core in range(2):
            auxes.append(remote(hbm, buf.at[3 - 3 * q], aux_send.at[n, 1 + core], aux_recv.at[n, 3 - 3 * q], (m, far + core)))

    def ob_group(n, k):
        w, size = GROUPS[n]
        core = w // 5
        kk = lax.rem(k + m + 2, 8)
        gd = lax.rem(8 * i + kk + 2 - w // 2 + 256, 256)
        md, td = lax.rem(gd, 16), 2 * (gd // 16) + core
        src = ob_t.at[pl.ds(4 * (2 * kk + w % 2), 4 * size)]
        dst = obs.at[pl.ds(4 * (w - core), 4 * size), pl.ds(pl.multiple_of(16 * m, 16), 16)]

        def away():
            return remote(src, dst, ob_send.at[n, k], ob_recv.at[n], (md, td))

        def stay():
            return pltpu.make_async_copy(src, dst, ob_recv.at[n])

        return (md == m) & (td == i), away, stay

    def launch(unit):
        here, away, stay = unit

        @pl.when(here)
        def _():
            stay().start()

        @pl.when(jnp.logical_not(here))
        def _():
            away().start()

    def left(unit):
        here, away, stay = unit

        @pl.when(jnp.logical_not(here))
        def _():
            away().wait_send()

    def each(count, act):
        def body(j, c):
            act(j)
            return c

        lax.fori_loop(0, count, body, 0)

    for n in ORDER[:2]:
        each(8, lambda k: launch(ob_group(n, k)))
    for copy in own_tabs + tabs + owns + auxes:
        copy.start()
    for n in ORDER[2:]:
        each(8, lambda k: launch(ob_group(n, k)))

    load_st.wait()

    def turn_st(b, c):
        for k in range(8):
            st_t[8 * b + k] = st_in[pl.ds(8 * b + k, 16, stride=256), :]
        return c

    lax.fori_loop(0, 32, turn_st, 0)

    def st_unit(t, j):
        kk, core = lax.rem(j // 2 + m + 2, 8), lax.rem(j, 2)
        md, td = 8 * q + kk, 2 * z + core
        src = st_t.at[pl.ds(16 * (2 * kk + core) + 4 * STEP * t, 4 * STEP)]
        dst = xbuf.at[pl.ds(4 * STEP * t, 4 * STEP), pl.ds(pl.multiple_of(16 * m, 16), 16)]

        def away():
            return remote(src, dst, st_send.at[t, j], st_recv.at[t], (md, td))

        def stay():
            return pltpu.make_async_copy(src, dst, st_recv.at[t])

        return (md == m) & (td == i), away, stay

    for t in range(PER // STEP):
        each(16, lambda j: launch(st_unit(t, j)))

    for copy in own_tabs:
        copy.wait()
    for copy in tabs:
        copy.wait_recv()
    which = jnp.where(home, 0, 1)
    to_smem = []
    for n, (hbm, buf, smem) in enumerate(tables):
        to_smem.append(pltpu.make_async_copy(buf.at[which], smem, local_sem.at[5 + n]))
    for copy in to_smem:
        copy.start()
    for copy in to_smem:
        copy.wait()
    for n, (hbm, buf) in enumerate(((val_hbm, vals), (prec_hbm, precs))):
        for slot in range(4):
            pltpu.make_async_copy(hbm, buf.at[slot], aux_recv.at[n, slot]).wait()

    def landed(slot, size, sem):
        ref = obs.at[pl.ds(slot, size)]
        pltpu.make_async_copy(ref, ref, sem).wait()

    landed(16 * q, 8, ob_recv.at[5 * q])
    landed(8 + 16 * q, 8, ob_recv.at[1 + 3 * q])
    landed(16, 4, ob_recv.at[2 + q])
    pair = remote(obs.at[pl.ds(4 + 12 * q, 16)], obs.at[pl.ds(20 * q, 16)], pair_send.at[0], pair_recv.at[0], sib)
    pair.start()
    landed(20 - 20 * q, 16, pair_recv.at[0])

    def tile_step(t, c):
        row = 8 * lax.rem(g, 8) + 4 * q + t
        count = ctab_s[0, row]
        proj = jnp.zeros((MEMBERS, 128), F32)
        for s in range(SLOTS):
            batch = itab_s[s, row]
            place = lax.rem(batch - (8 * g - 16 + 4 * q) + 4096, 2048)
            place = jnp.clip(place, 0, WINDOW - 1)
            where = lax.rem(batch - (128 * z - 64) + 4096, 2048)
            where = jnp.clip(where, 0, 255)
            shard, line_b = where // 64, lax.rem(where, 64)
            prior = obs[place]
            value = vals[shard, pl.ds(line_b, 1), :]
            prec = precs[shard, pl.ds(line_b, 1), :]
            weight = jnp.where(s < count, ftab_s[s, row], 0.0)
            size = jnp.sqrt(prec * weight)
            ymean = jnp.mean(prior, axis=0, keepdims=True)
            scaled = (prior - ymean) * size
            proj = proj + scaled * ((value - ymean) * size)
            high, low = split(scaled)
            vh[:, 128 * s : 128 * (s + 1)] = high
            vl[:, 128 * s : 128 * (s + 1)] = low
        both = (vh[...], vl[...])
        gram = mul(both, both, NT)
        turn = transform(gram, jnp.sum(proj, axis=1, keepdims=True))
        high, low = split(turn)
        th[t] = high
        tl[t] = low
        return c

    def apply_step(t, c):
        turn_s = (th[t], tl[t])

        @pl.when(lax.rem(t, STEP) == 0)
        def _():
            whole = xbuf.at[pl.ds(4 * t, 4 * STEP)]
            pltpu.make_async_copy(whole, whole, st_recv.at[t // STEP]).wait()

        for half in range(2):
            x = jnp.concatenate([xbuf[4 * t + 2 * half], xbuf[4 * t + 2 * half + 1]], axis=1)
            moved = mul(turn_s, split(x))
            obuf[4 * t + 2 * half] = moved[:, :128]
            obuf[4 * t + 2 * half + 1] = moved[:, 128:]

        @pl.when(lax.rem(t, OSTEP) == OSTEP - 1)
        def _():
            each(16, lambda j: launch(out_unit(t // OSTEP, j)))

        return c

    def out_unit(t, j):
        md = lax.rem(j + m + 5, 16)
        row = 4 * (8 * lax.rem(g, 8) + 4 * q + OSTEP * t)
        src = obuf.at[pl.ds(4 * OSTEP * t, 4 * OSTEP), pl.ds(pl.multiple_of(16 * md, 16), 16)]
        dst = out_ref.at[pl.ds(row, 4 * OSTEP)]

        def away():
            return remote(src, dst, out_send.at[t, j], out_recv.at[0], (md, src_shard))

        def stay():
            return pltpu.make_async_copy(src, dst, out_recv.at[0])

        return (md == m) & home, away, stay

    lax.fori_loop(0, PER, tile_step, 0)
    lax.fori_loop(0, PER, apply_step, 0)

    for copy in tabs + auxes:
        copy.wait_send()
    pair.wait_send()
    for n in range(len(GROUPS)):
        each(8, lambda k: left(ob_group(n, k)))
    for t in range(PER // STEP):
        each(16, lambda j: left(st_unit(t, j)))
    for t in range(PER // OSTEP):
        each(16, lambda j: left(out_unit(t, j)))
    pltpu.make_async_copy(out_ref, out_ref, out_recv.at[0]).wait()


def turn_kernel(in_ref, out_ref):
    for k in range(16):
        out_ref[k] = in_ref[pl.ds(k, 256 // TURNS, stride=16), :]


def per_device(state, obs_prior, obs_value, obs_prec, tile_batches, tile_count, loc_weight):
    anywhere = pl.BlockSpec(memory_space=pl.ANY)
    dma = pltpu.SemaphoreType.DMA
    out = pl.pallas_call(
        kernel,
        out_shape=jax.ShapeDtypeStruct((256, 16, 128), F32),
        in_specs=[anywhere] * 7,
        out_specs=anywhere,
        scratch_shapes=[
            pltpu.VMEM((16 * 256, 128), F32),
            pltpu.VMEM((256, 16, 128), F32),
            pltpu.VMEM((16 * 64, 128), F32),
            pltpu.VMEM((64, 16, 128), F32),
            pltpu.VMEM((WINDOW, MEMBERS, 128), F32),
            pltpu.VMEM((16, MEMBERS, 128), F32),
            pltpu.VMEM((16, MEMBERS, 128), F32),
            pltpu.VMEM((4, 64, 128), F32),
            pltpu.VMEM((4, 64, 128), F32),
            pltpu.VMEM((2, SLOTS, 64), jnp.int32),
            pltpu.VMEM((2, 1, 64), jnp.int32),
            pltpu.VMEM((2, SLOTS, 64), F32),
            pltpu.SMEM((SLOTS, 64), jnp.int32),
            pltpu.SMEM((1, 64), jnp.int32),
            pltpu.SMEM((SLOTS, 64), F32),
            pltpu.VMEM((MEMBERS, SLOTS * 128), BF16),
            pltpu.VMEM((MEMBERS, SLOTS * 128), BF16),
            pltpu.VMEM((PER, MEMBERS, MEMBERS), BF16),
            pltpu.VMEM((PER, MEMBERS, MEMBERS), BF16),
            dma((8,)),
            dma((3,)),
            dma((3,)),
            dma((2, 3)),
            dma((2, 4)),
            dma((6, 8)),
            dma((6,)),
            dma((1,)),
            dma((1,)),
            dma((4, 16)),
            dma((4,)),
            dma((4, 16)),
            dma((1,)),
        ],
        compiler_params=pltpu.CompilerParams(collective_id=0, has_side_effects=True, vmem_limit_bytes=60 * 2**20),
        name="etkf",
    )(
        state.reshape(16 * 256, 128),
        obs_prior.reshape(16 * 64, 128),
        obs_value,
        obs_prec,
        tile_batches.T,
        tile_count.reshape(1, 64),
        loc_weight.T,
    )
    turned = pl.pallas_call(
        turn_kernel,
        grid=(TURNS,),
        out_shape=jax.ShapeDtypeStruct((16, 256, 128), F32),
        in_specs=[pl.BlockSpec((16 * 256 // TURNS, 128), lambda b: (b, 0))],
        out_specs=pl.BlockSpec((16, 256 // TURNS, 128), lambda b: (0, b, 0)),
        compiler_params=pltpu.CompilerParams(vmem_limit_bytes=60 * 2**20),
        name="turn",
    )(out.reshape(256 * 16, 128))
    return turned.reshape(16, 64, 4, 128)


def solution(mesh):
    in_specs = (
        P("mem", "tile", None, None),
        P("mem", "tile", None),
        P("tile", None),
        P("tile", None),
        P("tile", None),
        P("tile"),
        P("tile", None),
    )
    out_specs = P("mem", "tile", None, None)
    return jax.shard_map(
        per_device, mesh=mesh, in_specs=in_specs, out_specs=out_specs, check_vma=False
    )
```

```python
import jax
import jax.numpy as jnp
from jax import lax
from jax.experimental import pallas as pl
from jax.experimental.pallas import tpu as pltpu
from jax.sharding import PartitionSpec as P

MESH = pl.DeviceIdType.MESH
MEMBERS = 256
SLOTS = 6
PER = 4
WINDOW = 36
STEP = 1
OSTEP = 1
TURNS = 2
GROUPS = ((0, 2), (2, 2), (4, 1), (5, 1), (6, 2), (8, 2))
ORDER = (2, 3, 1, 4, 0, 5)

F32 = jnp.float32
BF16 = jnp.bfloat16
NN = (((1,), (0,)), ((), ()))
NT = (((1,), (1,)), ((), ()))


def split(x):
    high = x.astype(BF16)
    return high, (x - high.astype(F32)).astype(BF16)


def mxu(a, b, dims=NN):
    return lax.dot_general(a, b, dims, preferred_element_type=F32)


def mul(a, b, dims=NN):
    ah, al = a
    bh, bl = b
    return mxu(ah, bh, dims) + (mxu(ah, bl, dims) + mxu(al, bh, dims))


def transform(gram, proj):
    rows = lax.broadcasted_iota(jnp.int32, (MEMBERS, MEMBERS), 0)
    cols = lax.broadcasted_iota(jnp.int32, (MEMBERS, MEMBERS), 1)
    diag = rows == cols
    ident = diag.astype(F32)
    amat = (MEMBERS - 1.0) * ident + gram
    scale = jnp.sqrt(jnp.sum(amat * amat, keepdims=True))
    root = amat * (1.0 / scale)
    first = 1.5 * ident - 0.5 * root
    root_s = split(root)
    first_s = split(first)
    square = mul(root_s, root_s)
    inner = mul(first_s, split(1.5 * root - 0.5 * square))
    second = 1.5 * ident - 0.5 * inner
    second_s = split(second)
    r = mul(second_s, second_s)
    poly = 1.5 * second + mul(split(r), split(r - 1.5 * second))
    inverse = mul(first_s, split(poly))
    once = jnp.sum(inverse * proj, axis=0, keepdims=True)
    twice = jnp.sum(inverse * once, axis=1, keepdims=True) * (1.0 / scale)
    wmean = jnp.sum(jnp.where(diag, twice, 0.0), axis=0, keepdims=True)
    full = jnp.sqrt((MEMBERS - 1.0) / scale) * inverse + wmean
    return full - jnp.mean(full, axis=1, keepdims=True) + 1.0 / MEMBERS


def kernel(
    st_hbm, ob_hbm, val_hbm, prec_hbm, itab_hbm, ctab_hbm, ftab_hbm,
    out_ref,
    st_in, st_t, ob_in, ob_t, obs, xbuf, obuf, vals, precs, itab, ctab, ftab, itab_s, ctab_s, ftab_s,
    vh, vl, th, tl, local_sem, tab_send, tab_recv, aux_send, aux_recv, ob_send, ob_recv, pair_send, pair_recv, st_send, st_recv, out_send, out_recv,
):
    m = lax.axis_index("mem")
    i = lax.axis_index("tile")
    q = lax.rem(i, 2)
    z = i // 2
    g = 16 * z + m
    sib = (m, i + 1 - 2 * q)
    src_shard = g // 8
    home = src_shard == i

    load_ob = pltpu.make_async_copy(ob_hbm, ob_in, local_sem.at[0])
    load_st = pltpu.make_async_copy(st_hbm, st_in, local_sem.at[1])
    load_ob.start()
    load_st.start()

    barrier = pltpu.get_barrier_semaphore()

    def greet(device):
        pl.semaphore_signal(barrier, inc=1, device_id=device, device_id_type=MESH)

    def greet_source(j, c):
        @pl.when(jnp.logical_not(home & (j == m)))
        def _():
            greet((j, src_shard))
        return c

    def greet_owner(j, c):
        md, td = 8 * q + j // 2, 2 * z + lax.rem(j, 2)

        @pl.when(jnp.logical_not((md == m) & (td == i)))
        def _():
            greet((md, td))
        return c

    def greet_edge(j, c):
        greet((j, lax.rem(src_shard + 2 * q - 1 + 32, 32)))
        return c

    lax.fori_loop(0, 16, greet_source, 0)
    lax.fori_loop(0, 16, greet_owner, 0)
    edge = ((q == 0) & (lax.rem(g, 8) <= 1)) | ((q == 1) & (lax.rem(g, 8) >= 6))

    @pl.when(edge)
    def _():
        lax.fori_loop(0, 16, greet_edge, 0)

    greet(sib)
    greet((m, lax.rem(2 * z + 31, 32)))
    greet((m, lax.rem(2 * z + 2, 32)))

    load_ob.wait()

    def turn_ob(b, c):
        for k in range(4):
            ob_t[4 * b + k] = ob_in[pl.ds(4 * b + k, 16, stride=64), :]
        return c

    lax.fori_loop(0, 16, turn_ob, 0)

    @pl.when(home)
    def _():
        pl.semaphore_wait(barrier, 37)

    @pl.when(jnp.logical_not(home))
    def _():
        pl.semaphore_wait(barrier, 39)

    def remote(src, dst, ss, rs, device):
        return pltpu.make_async_remote_copy(src_ref=src, dst_ref=dst, send_sem=ss, recv_sem=rs, device_id=device, device_id_type=MESH)

    tables = ((itab_hbm, itab, itab_s), (ctab_hbm, ctab, ctab_s), (ftab_hbm, ftab, ftab_s))
    own_tabs, tabs = [], []
    for n, (hbm, buf, smem) in enumerate(tables):
        own_tabs.append(pltpu.make_async_copy(hbm, buf.at[0], local_sem.at[2 + n]))
        tabs.append(remote(hbm, buf.at[1], tab_send.at[n], tab_recv.at[n], sib))
    far = 2 * lax.rem(z + 2 * q - 1 + 16, 16)
    auxes = []
    owns = []
    for n, (hbm, buf) in enumerate(((val_hbm, vals), (prec_hbm, precs))):
        owns.append(pltpu.make_async_copy(hbm, buf.at[q + 1], aux_recv.at[n, q + 1]))
        auxes.append(remote(hbm, buf.at[q + 1], aux_send.at[n, 0], aux_recv.at[n, q + 1], sib))
        for core in range(2):
            auxes.append(remote(hbm, buf.at[3 - 3 * q], aux_send.at[n, 1 + core], aux_recv.at[n, 3 - 3 * q], (m, far + core)))

    def ob_group(n, k):
        w, size = GROUPS[n]
        core = w // 5
        kk = lax.rem(k + m + 2, 8)
        gd = lax.rem(8 * i + kk + 2 - w // 2 + 256, 256)
        md, td = lax.rem(gd, 16), 2 * (gd // 16) + core
        src = ob_t.at[pl.ds(4 * (2 * kk + w % 2), 4 * size)]
        dst = obs.at[pl.ds(4 * (w - core), 4 * size), pl.ds(pl.multiple_of(16 * m, 16), 16)]

        def away():
            return remote(src, dst, ob_send.at[n, k], ob_recv.at[n], (md, td))

        def stay():
            return pltpu.make_async_copy(src, dst, ob_recv.at[n])

        return (md == m) & (td == i), away, stay

    def launch(unit):
        here, away, stay = unit

        @pl.when(here)
        def _():
            stay().start()

        @pl.when(jnp.logical_not(here))
        def _():
            away().start()

    def left(unit):
        here, away, stay = unit

        @pl.when(jnp.logical_not(here))
        def _():
            away().wait_send()

    def each(count, act):
        def body(j, c):
            act(j)
            return c

        lax.fori_loop(0, count, body, 0)

    for n in ORDER[:2]:
        each(8, lambda k: launch(ob_group(n, k)))
    for copy in own_tabs + tabs + owns + auxes:
        copy.start()
    for n in ORDER[2:]:
        each(8, lambda k: launch(ob_group(n, k)))

    load_st.wait()

    def turn_st(b, c):
        for k in range(8):
            st_t[8 * b + k] = st_in[pl.ds(8 * b + k, 16, stride=256), :]
        return c

    lax.fori_loop(0, 32, turn_st, 0)

    def st_unit(t, j):
        kk, core = lax.rem(j // 2 + m + 2, 8), lax.rem(j, 2)
        md, td = 8 * q + kk, 2 * z + core
        src = st_t.at[pl.ds(16 * (2 * kk + core) + 4 * STEP * t, 4 * STEP)]
        dst = xbuf.at[pl.ds(4 * STEP * t, 4 * STEP), pl.ds(pl.multiple_of(16 * m, 16), 16)]

        def away():
            return remote(src, dst, st_send.at[t, j], st_recv.at[t], (md, td))

        def stay():
            return pltpu.make_async_copy(src, dst, st_recv.at[t])

        return (md == m) & (td == i), away, stay

    for t in range(PER // STEP):
        each(16, lambda j: launch(st_unit(t, j)))

    for copy in own_tabs:
        copy.wait()
    for copy in tabs:
        copy.wait_recv()
    which = jnp.where(home, 0, 1)
    to_smem = []
    for n, (hbm, buf, smem) in enumerate(tables):
        to_smem.append(pltpu.make_async_copy(buf.at[which], smem, local_sem.at[5 + n]))
    for copy in to_smem:
        copy.start()
    for copy in to_smem:
        copy.wait()
    for n, (hbm, buf) in enumerate(((val_hbm, vals), (prec_hbm, precs))):
        for slot in range(4):
            pltpu.make_async_copy(hbm, buf.at[slot], aux_recv.at[n, slot]).wait()

    def landed(slot, size, sem):
        ref = obs.at[pl.ds(slot, size)]
        pltpu.make_async_copy(ref, ref, sem).wait()

    landed(16 * q, 8, ob_recv.at[5 * q])
    landed(8 + 16 * q, 8, ob_recv.at[1 + 3 * q])
    landed(16, 4, ob_recv.at[2 + q])
    pair = remote(obs.at[pl.ds(4 + 12 * q, 16)], obs.at[pl.ds(20 * q, 16)], pair_send.at[0], pair_recv.at[0], sib)
    pair.start()
    landed(20 - 20 * q, 16, pair_recv.at[0])

    def tile_step(t, c):
        row = 8 * lax.rem(g, 8) + 4 * q + t
        count = ctab_s[0, row]
        proj = jnp.zeros((MEMBERS, 128), F32)
        for s in range(SLOTS):
            batch = itab_s[s, row]
            place = lax.rem(batch - (8 * g - 16 + 4 * q) + 4096, 2048)
            place = jnp.clip(place, 0, WINDOW - 1)
            where = lax.rem(batch - (128 * z - 64) + 4096, 2048)
            where = jnp.clip(where, 0, 255)
            shard, line_b = where // 64, lax.rem(where, 64)
            prior = obs[place]
            value = vals[shard, pl.ds(line_b, 1), :]
            prec = precs[shard, pl.ds(line_b, 1), :]
            weight = jnp.where(s < count, ftab_s[s, row], 0.0)
            size = jnp.sqrt(prec * weight)
            ymean = jnp.mean(prior, axis=0, keepdims=True)
            scaled = (prior - ymean) * size
            proj = proj + scaled * ((value - ymean) * size)
            high, low = split(scaled)
            vh[:, 128 * s : 128 * (s + 1)] = high
            vl[:, 128 * s : 128 * (s + 1)] = low
        both = (vh[...], vl[...])
        gram = mul(both, both, NT)
        turn = transform(gram, jnp.sum(proj, axis=1, keepdims=True))
        high, low = split(turn)
        th[t] = high
        tl[t] = low
        return c

    def apply_step(t, c):
        turn_s = (th[t], tl[t])

        @pl.when(lax.rem(t, STEP) == 0)
        def _():
            whole = xbuf.at[pl.ds(4 * t, 4 * STEP)]
            pltpu.make_async_copy(whole, whole, st_recv.at[t // STEP]).wait()

        for half in range(2):
            x = jnp.concatenate([xbuf[4 * t + 2 * half], xbuf[4 * t + 2 * half + 1]], axis=1)
            moved = mul(turn_s, split(x))
            obuf[4 * t + 2 * half] = moved[:, :128]
            obuf[4 * t + 2 * half + 1] = moved[:, 128:]

        @pl.when(lax.rem(t, OSTEP) == OSTEP - 1)
        def _():
            each(16, lambda j: launch(out_unit(t // OSTEP, j)))

        return c

    def out_unit(t, j):
        md = lax.rem(m + 32 + (1 - 2 * q) * (j + 5), 16)
        row = 4 * (8 * lax.rem(g, 8) + 4 * q + OSTEP * t)
        src = obuf.at[pl.ds(4 * OSTEP * t, 4 * OSTEP), pl.ds(pl.multiple_of(16 * md, 16), 16)]
        dst = out_ref.at[pl.ds(row, 4 * OSTEP)]

        def away():
            return remote(src, dst, out_send.at[t, j], out_recv.at[0], (md, src_shard))

        def stay():
            return pltpu.make_async_copy(src, dst, out_recv.at[0])

        return (md == m) & home, away, stay

    lax.fori_loop(0, PER, tile_step, 0)
    lax.fori_loop(0, PER, apply_step, 0)

    for copy in tabs + auxes:
        copy.wait_send()
    pair.wait_send()
    for n in range(len(GROUPS)):
        each(8, lambda k: left(ob_group(n, k)))
    for t in range(PER // STEP):
        each(16, lambda j: left(st_unit(t, j)))
    for t in range(PER // OSTEP):
        each(16, lambda j: left(out_unit(t, j)))
    pltpu.make_async_copy(out_ref, out_ref, out_recv.at[0]).wait()


def turn_kernel(in_ref, out_ref):
    for k in range(16):
        out_ref[k] = in_ref[pl.ds(k, 256 // TURNS, stride=16), :]


def per_device(state, obs_prior, obs_value, obs_prec, tile_batches, tile_count, loc_weight):
    anywhere = pl.BlockSpec(memory_space=pl.ANY)
    dma = pltpu.SemaphoreType.DMA
    out = pl.pallas_call(
        kernel,
        out_shape=jax.ShapeDtypeStruct((256, 16, 128), F32),
        in_specs=[anywhere] * 7,
        out_specs=anywhere,
        scratch_shapes=[
            pltpu.VMEM((16 * 256, 128), F32),
            pltpu.VMEM((256, 16, 128), F32),
            pltpu.VMEM((16 * 64, 128), F32),
            pltpu.VMEM((64, 16, 128), F32),
            pltpu.VMEM((WINDOW, MEMBERS, 128), F32),
            pltpu.VMEM((16, MEMBERS, 128), F32),
            pltpu.VMEM((16, MEMBERS, 128), F32),
            pltpu.VMEM((4, 64, 128), F32),
            pltpu.VMEM((4, 64, 128), F32),
            pltpu.VMEM((2, SLOTS, 64), jnp.int32),
            pltpu.VMEM((2, 1, 64), jnp.int32),
            pltpu.VMEM((2, SLOTS, 64), F32),
            pltpu.SMEM((SLOTS, 64), jnp.int32),
            pltpu.SMEM((1, 64), jnp.int32),
            pltpu.SMEM((SLOTS, 64), F32),
            pltpu.VMEM((MEMBERS, SLOTS * 128), BF16),
            pltpu.VMEM((MEMBERS, SLOTS * 128), BF16),
            pltpu.VMEM((PER, MEMBERS, MEMBERS), BF16),
            pltpu.VMEM((PER, MEMBERS, MEMBERS), BF16),
            dma((8,)),
            dma((3,)),
            dma((3,)),
            dma((2, 3)),
            dma((2, 4)),
            dma((6, 8)),
            dma((6,)),
            dma((1,)),
            dma((1,)),
            dma((4, 16)),
            dma((4,)),
            dma((4, 16)),
            dma((1,)),
        ],
        compiler_params=pltpu.CompilerParams(collective_id=0, has_side_effects=True, vmem_limit_bytes=60 * 2**20),
        name="etkf",
    )(
        state.reshape(16 * 256, 128),
        obs_prior.reshape(16 * 64, 128),
        obs_value,
        obs_prec,
        tile_batches.T,
        tile_count.reshape(1, 64),
        loc_weight.T,
    )
    turned = pl.pallas_call(
        turn_kernel,
        grid=(TURNS,),
        out_shape=jax.ShapeDtypeStruct((16, 256, 128), F32),
        in_specs=[pl.BlockSpec((16 * 256 // TURNS, 128), lambda b: (b, 0))],
        out_specs=pl.BlockSpec((16, 256 // TURNS, 128), lambda b: (0, b, 0)),
        compiler_params=pltpu.CompilerParams(vmem_limit_bytes=60 * 2**20),
        name="turn",
    )(out.reshape(256 * 16, 128))
    return turned.reshape(16, 64, 4, 128)


def solution(mesh):
    in_specs = (
        P("mem", "tile", None, None),
        P("mem", "tile", None),
        P("tile", None),
        P("tile", None),
        P("tile", None),
        P("tile"),
        P("tile", None),
    )
    out_specs = P("mem", "tile", None, None)
    return jax.shard_map(
        per_device, mesh=mesh, in_specs=in_specs, out_specs=out_specs, check_vma=False
    )
```
